256 devices in a mesh: span: 16 (over x, y_lo, core), sp: 16 (over z, y_hi).
Axes of the slice: x: 4, y: 4 (y_hi: 2, y_lo: 2; y = y_hi * 2 + y_lo), z: 8, core: 2. Of those that a mesh axis runs over, the one named last changes fastest.
Arguments:
- queries: bfloat16 [16, 2048, 3072], P('span', 'sp'), may hold values from -8 to 8
- keys: bfloat16 [16, 2048, 3072], P('span', 'sp'), may hold values from -8 to 8
- values: bfloat16 [16, 2048, 3072], P('span', 'sp'), may hold values from -6 to 6
- cache_keys: bfloat16 [16, 2048, 3072], P('span', None, 'sp'), may hold values from -8 to 8
- cache_values: bfloat16 [16, 2048, 3072], P('span', None, 'sp'), may hold values from -6 to 6
- gate_table: float32 [64, 3072], replicated, may hold values from 0.5 to 2
- prefix_len: int32 [16], P('span'), may hold values from 1 to 2048, as said below
- levels: int32 [16], P('span'), may hold values from 0 to 63
- finisher: int32 [16], replicated, may hold values from 0 to 15, as said below
Outputs:
- attended: bfloat16 [16, 2048, 3072], P('span', 'sp')
The draws below stay inside these ranges and needn't reach their ends.
Inputs may be any that keep to these rules, and one draw needn't show every extreme that they name: `prefix_len`: the last group's cache is full. `finisher`: a permutation of the 16 group indices whose first entry is below 15.
All inputs are finite; a program needn't handle non-finite values.
Results may differ from the reference program's by a relative error of at most 0.0032.
Values may be sent and summed in bfloat16 or wider, within the bound.
A program may use at most 128 MiB of HBM per device.

```python
import jax
import jax.numpy as jnp
from jax import lax

H = 48
HD = 64
D = 3072
CT = 2048
CACHE = 2048
LEVELS = 64
GROUPS = 16


def draw_queries(key, part):
    key = jax.random.fold_in(key, 3)
    base = jnp.clip(2.0 * jax.random.normal(key, (GROUPS, CT, D), jnp.float32), -8.0, 8.0)
    return base.astype(jnp.bfloat16)


def draw_keys(key, part):
    key = jax.random.fold_in(key, 5)
    base = jnp.clip(1.25 * jax.random.normal(key, (GROUPS, CT, D), jnp.float32), -8.0, 8.0)
    return base.astype(jnp.bfloat16)


def draw_prefix_len(key, part):
    key = jax.random.fold_in(key, 7)
    group_index = jnp.arange(GROUPS, dtype=jnp.int32)
    base = (group_index + 1) * CACHE // GROUPS
    dropped = jax.random.randint(key, (GROUPS,), 0, CACHE // (2 * GROUPS) + 1, dtype=jnp.int32)
    length = jnp.maximum(base - dropped, 1)
    return jnp.where(group_index == GROUPS - 1, CACHE, length).astype(jnp.int32)


def draw_finisher(key, part):
    key = jax.random.fold_in(key, 11)
    order = jax.random.permutation(key, jnp.arange(GROUPS, dtype=jnp.int32))
    first = order[0]
    second = order[1]
    swapped = first == GROUPS - 1
    order = order.at[0].set(jnp.where(swapped, second, first))
    order = order.at[1].set(jnp.where(swapped, first, second))
    return order.astype(jnp.int32)


def place_ends(array, rng, low, largest):
    index_at = [jax.random.randint(jax.random.fold_in(rng, axis), (), 0, length) for axis, length in enumerate(array.shape)]
    widest = array.shape.index(max(array.shape))
    neighbour = index_at[:widest] + [(index_at[widest] + 1) % array.shape[widest]] + index_at[widest + 1:]
    return array.at[tuple(index_at)].set(low).at[tuple(neighbour)].set(largest)


def level_of(stream_key, dims, cuts, low, high):
    def one(dim, blocks):
        steps = jax.random.uniform(jax.random.fold_in(jax.random.fold_in(stream_key, 6), dim), (blocks,), jnp.float32, low / len(cuts), high / len(cuts))
        return jnp.repeat(jnp.exp(steps), dims[dim] // blocks).reshape((-1,) + (1,) * (len(dims) - dim - 1))

    factor_of = one(*cuts[0])
    for cut in cuts[1:]:
        factor_of = factor_of * one(*cut)
    return factor_of


def centred(rng, extent, spread, reach, split=(), kind=jnp.bfloat16):
    factor_of = level_of(rng, extent, split, -0.22, 0.18) if split else 1.0
    entries = jax.random.normal(rng, extent, jnp.float32) * spread * factor_of
    return jnp.minimum(jnp.maximum(entries, -reach), reach).astype(kind)


def setup_inputs(seed: int = 0) -> dict:
    key_list = jax.random.split(jax.random.key(seed), 10)
    return {
        "queries": draw_queries(jax.random.fold_in(key_list[9], 71), 0),
        "keys": draw_keys(jax.random.fold_in(key_list[9], 71), 0),
        "values": centred(key_list[2], (GROUPS, CT, D), 1.0, 6.0, ((0, 16), (1, 16))),
        "cache_keys": centred(key_list[3], (GROUPS, CACHE, D), 1.25, 8.0, ((0, 16), (2, 16))),
        "cache_values": centred(key_list[4], (GROUPS, CACHE, D), 1.0, 6.0, ((0, 16), (2, 16))),
        "gate_table": jnp.clip(jax.random.uniform(key_list[5], (LEVELS, D), jnp.float32, 0.5, 2.0), 0.5, 2.0),
        "prefix_len": draw_prefix_len(jax.random.fold_in(key_list[9], 71), 0),
        "levels": place_ends(jax.random.randint(key_list[7], (GROUPS,), 0, LEVELS), jax.random.fold_in(key_list[7], 1), 0, LEVELS - 1).astype(jnp.int32),
        "finisher": draw_finisher(jax.random.fold_in(key_list[9], 71), 0),
    }


def head_attend(query_rows, key_rows, value_rows, usable, score_scale):
    scores = jnp.dot(query_rows, key_rows.T, preferred_element_type=jnp.float32) * score_scale
    row_max = jnp.max(jnp.where(usable[None, :], scores, -jnp.inf), axis=1, keepdims=True)
    weights = jnp.where(usable[None, :], jnp.exp(scores - row_max), jnp.float32(0.0))
    row_sum = jnp.sum(weights, axis=1, keepdims=True)
    blended = jnp.dot(weights.astype(jnp.bfloat16), value_rows, preferred_element_type=jnp.float32)
    return blended / row_sum


def reference(queries, keys, values, cache_keys, cache_values, gate_table, prefix_len, levels, finisher):
    chosen = finisher[0]
    score_scale = HD ** -0.5
    newest_keys = lax.dynamic_index_in_dim(keys, chosen, 0, False)
    newest_values = lax.dynamic_index_in_dim(values, chosen, 0, False)
    positions = jnp.arange(CACHE, dtype=jnp.int32)

    def one_group(members):
        group_index, query_rows, own_keys, own_values, old_keys, old_values, length, noise_level = members
        usable = jnp.concatenate([positions < length, jnp.full((CT,), group_index > chosen), jnp.ones((CT,), bool)])
        key_rows = jnp.concatenate([old_keys, newest_keys, own_keys], 0)
        value_rows = jnp.concatenate([old_values, newest_values, own_values], 0)
        key_heads = key_rows.reshape(-1, H, HD).transpose(1, 0, 2)
        value_heads = value_rows.reshape(-1, H, HD).transpose(1, 0, 2)
        query_heads = query_rows.reshape(CT, H, HD).transpose(1, 0, 2)
        blended = lax.map(lambda parts: head_attend(parts[0], parts[1], parts[2], usable, score_scale),
                          (query_heads, key_heads, value_heads))
        blended = blended.transpose(1, 0, 2).reshape(CT, D)
        gate_row = lax.dynamic_index_in_dim(gate_table, noise_level, 0, False)
        return (blended * gate_row).astype(jnp.bfloat16)

    return lax.map(one_group, (jnp.arange(GROUPS, dtype=jnp.int32), queries, keys, values,
                               cache_keys, cache_values, prefix_len, levels))
```

```python
import functools
import math

import jax
import jax.numpy as jnp
from jax import lax
from jax.experimental import pallas as pl
from jax.experimental.pallas import tpu as pltpu
from jax.sharding import PartitionSpec as P

MESH = pl.DeviceIdType.MESH
N = 16
TB = 128
HL = 3
ROWS = 2048
D = 3072
BF = jnp.bfloat16
F32 = jnp.float32
SCALE = 64 ** -0.5 * math.log2(math.e)
BQ = 1024
BK = 1024
NEG = -1e30


def swap(x):
    return jnp.concatenate([x[..., 64:], x[..., :64]], axis=-1)


def low_lanes(shape):
    return lax.broadcasted_iota(jnp.int32, shape, len(shape) - 1) < 64


def kernel(
    q_hbm, k_hbm, v_hbm, ck_hbm, cv_hbm, gate_hbm, plen_ref, level_ref, fin_ref, o_ref,
    q_in, k_in, v_in, ck_in, cv_in, gate_in, gate_row,
    q_pack, kv_pack, q_got, kv_got, kv8, near, pick, part, span_pack, span_got,
    qx, kx, vx, acc_ref, max_ref, out_pack, out_got,
    in_sem, qs, qr, kvs, kvr, s1, r1, s2, r2, s3, r3, os, orr,
):
    sp = lax.axis_index("sp")
    g = lax.axis_index("span")
    newest = fin_ref[0]

    def sp_peer(d):
        return lax.rem(sp + d, N)

    def span_peer(d):
        return lax.rem(g + d, N)

    barrier = pltpu.get_barrier_semaphore()

    def greet(d, _):
        pl.semaphore_signal(barrier, inc=1, device_id={"sp": sp_peer(d)}, device_id_type=MESH)
        pl.semaphore_signal(barrier, inc=1, device_id={"span": span_peer(d)}, device_id_type=MESH)
        return 0

    lax.fori_loop(1, N, greet, 0)

    loads = [
        pltpu.make_async_copy(src, dst, in_sem.at[i])
        for i, (src, dst) in enumerate(
            [
                (q_hbm.at[0], q_in),
                (k_hbm.at[0], k_in),
                (v_hbm.at[0], v_in),
                (ck_hbm.at[0], ck_in),
                (cv_hbm.at[0], cv_in),
                (gate_hbm, gate_in),
            ]
        )
    ]
    for load in loads:
        load.start()

    def wait_bytes(ref, sem):
        pltpu.make_async_copy(ref, ref, sem).wait()

    def to_sp(src_of, dst, send, recv):
        def body(d, _):
            to = sp_peer(d)
            pltpu.make_async_remote_copy(
                src_ref=src_of(to), dst_ref=dst, send_sem=send, recv_sem=recv,
                device_id={"sp": to}, device_id_type=MESH,
            ).start()
            return 0

        lax.fori_loop(1, N, body, 0)

    def to_span(src_of, dst, send, recv):
        def body(d, _):
            to = span_peer(d)
            pltpu.make_async_remote_copy(
                src_ref=src_of(to), dst_ref=dst, send_sem=send, recv_sem=recv,
                device_id={"span": to}, device_id_type=MESH,
            ).start()
            return 0

        lax.fori_loop(1, N, body, 0)

    loads[0].wait()
    low = low_lanes((64, 128))
    for t in range(D // 128):
        x = q_in[:, t * 128 : (t + 1) * 128].astype(F32)
        first, second = x[:64], x[64:]
        even = jnp.where(low, first, swap(second)).astype(BF)
        odd = jnp.where(low, swap(first), second).astype(BF)
        for j, value in ((2 * t, even), (2 * t + 1, odd)):
            q_pack[j % HL, j // HL] = value
    for h in range(HL):
        q_got[h, sp] = q_pack[h, sp]
    pl.semaphore_wait(barrier, 2 * (N - 1))
    for h in range(HL):
        to_sp(lambda to: q_pack.at[h, to], q_got.at[h, sp], qs.at[h], qr.at[h])

    loads[1].wait()
    loads[2].wait()
    low = low_lanes((TB, 128))
    for t in range(D // 128):
        k = k_in[:, t * 128 : (t + 1) * 128].astype(F32)
        v = v_in[:, t * 128 : (t + 1) * 128].astype(F32)
        even = jnp.where(low, k, swap(v)).astype(BF)
        odd = jnp.where(low, swap(k), v).astype(BF)
        for j, value in ((2 * t, even), (2 * t + 1, odd)):
            kv_pack[j % HL, j // HL] = value
    for h in range(HL):
        kv_got[h, sp] = kv_pack[h, sp]

    def send_kv(h):
        to_sp(lambda to: kv_pack.at[h, to], kv_got.at[h, sp], kvs.at[h], kvr.at[h])

    send_kv(0)

    def eight(i, _):
        rows = pl.ds(pl.multiple_of(i * 16, 16), 16)
        k = k_in[rows, :].astype(F32)
        v = v_in[rows, :].astype(F32)
        kv8[2 * i] = jnp.concatenate([k[:8], v[:8]], axis=0).astype(BF)
        kv8[2 * i + 1] = jnp.concatenate([k[8:], v[8:]], axis=0).astype(BF)
        return 0

    lax.fori_loop(0, N // 2, eight, 0)
    near[g] = kv8[g]
    to_span(lambda to: kv8.at[to], near.at[g], s1, r1)

    loads[5].wait()
    low1 = low_lanes((1, 128))
    for h in range(HL):
        j = sp * HL + h
        tile = pl.ds(pl.multiple_of(lax.div(j, 2) * 128, 128), 128)
        chosen = lax.broadcasted_iota(jnp.int32, (64, 128), 0) == level_ref[0]
        row = jnp.sum(jnp.where(chosen, gate_in[:, tile], 0.0), axis=0, keepdims=True)
        odd = lax.rem(j, 2)
        gate_row[h] = jnp.where(jnp.zeros((1, 128), jnp.int32) + odd == 1, swap(row), row)

    loads[3].wait()
    loads[4].wait()
    CH = 256
    low = low_lanes((CH, 128))

    def cache_keys_of(x0, x2, mask):
        r0 = swap(x0)
        return [
            jnp.where(mask, x0, r0),
            jnp.where(mask, r0, x0),
            jnp.concatenate([x2, x2], axis=1),
        ]

    first0 = ck_in[0:16, 0:128].astype(F32)[0:1]
    first2 = ck_in[0:16, 128:192].astype(F32)[0:1]
    first_row = cache_keys_of(first0, first2, low1)

    def cache(i, _):
        rows = pl.ds(pl.multiple_of(i * CH, CH), CH)
        valid = lax.broadcasted_iota(jnp.int32, (CH, 128), 0) + i * CH < plen_ref[0]
        keys = cache_keys_of(ck_in[rows, 0:128].astype(F32), ck_in[rows, 128:192].astype(F32), low)
        v0 = cv_in[rows, 0:128].astype(F32)
        v2 = cv_in[rows, 128:192].astype(F32)
        values = [
            jnp.where(low, v0, 1.0),
            jnp.where(low, swap(v0), 1.0),
            jnp.concatenate([v2, jnp.ones_like(v2)], axis=1),
        ]
        for h in range(HL):
            kx[h, 0, rows, :] = jnp.where(valid, keys[h], first_row[h]).astype(BF)
            vx[h, 0, rows, :] = jnp.where(valid, values[h], 0.0).astype(BF)
        return 0

    lax.fori_loop(0, ROWS // CH, cache, 0)

    def clear(h, _):
        acc_ref[h] = jnp.zeros((ROWS, 128), F32)
        max_ref[h] = jnp.full((ROWS, 128), NEG, F32)
        return 0

    lax.fori_loop(0, HL, clear, 0)

    def take_queries(h):
        wait_bytes(q_got.at[h, pl.ds(0, N - 1)], qr.at[h])
        mask = low_lanes((64, 128))

        def body(b, _):
            x = q_got[h, b].astype(F32) * SCALE
            r = swap(x)

            def pair(top, bottom):
                rest = bottom - bottom.astype(BF).astype(F32)
                return jnp.where(mask, top, rest).astype(BF)

            qx[h, b, 0:64] = pair(x, r)
            qx[h, b, 64:128] = pair(r, x)
            return 0

        lax.fori_loop(0, N, body, 0)

    def take_own(h):
        wait_bytes(kv_got.at[h, pl.ds(0, N - 1)], kvr.at[h])
        mask = low_lanes((TB, 128))

        def body(b, _):
            x = kv_got[h, b].astype(F32)
            r = swap(x)
            rows = pl.ds(pl.multiple_of(b * TB, TB), TB)
            kx[h, 1, rows, :] = jnp.where(mask, x, r).astype(BF)
            vx[h, 1, rows, :] = jnp.where(mask, r, 1.0).astype(BF)
            return 0

        lax.fori_loop(0, N, body, 0)

    def take_newest(h):
        wait_bytes(span_got.at[h, pl.ds(0, N - 1)], r3.at[h])
        mask = low_lanes((TB, 128))
        used = jnp.zeros((TB, 128), jnp.int32) + g > newest
        spare = kx[h, 0, 0:16, :].astype(F32)[0:1]

        def body(b, _):
            x = span_got[h, b].astype(F32)
            r = swap(x)
            rows = pl.ds(pl.multiple_of(b * TB, TB), TB)
            kx[h, 2, rows, :] = jnp.where(used, jnp.where(mask, x, r), spare).astype(BF)
            vx[h, 2, rows, :] = jnp.where(used, jnp.where(mask, r, 1.0), 0.0).astype(BF)
            return 0

        lax.fori_loop(0, N, body, 0)

    def window(s):
        return pl.ds(pl.multiple_of(lax.div(s * HL, 2) * 128, 128), 256)

    def pick_newest():
        wait_bytes(near.at[pl.ds(0, N - 1)], r1)

        def choose(j, kept):
            chosen = jnp.zeros((16, D), jnp.int32) + newest == j
            return jnp.where(chosen, near[j].astype(F32), kept)

        pick[...] = lax.fori_loop(0, N, choose, jnp.zeros((16, D), F32)).astype(BF)
        part[sp] = pick[:, window(sp)]
        to_sp(lambda to: pick.at[:, window(to)], part.at[sp], s2, r2)

    def spread_newest():
        wait_bytes(part.at[pl.ds(0, N - 1)], r2)
        x = part[...].astype(F32)
        k = x[:, :8].reshape(TB, 256)
        v = x[:, 8:].reshape(TB, 256)
        odd = jnp.zeros((TB, 64), jnp.int32) + lax.rem(sp, 2) == 1

        def piece(y, h):
            return jnp.where(odd, y[:, 64 * (h + 1) : 64 * (h + 2)], y[:, 64 * h : 64 * (h + 1)])

        for h in range(HL):
            value = jnp.concatenate([piece(k, h), piece(v, h)], axis=1).astype(BF)
            span_pack[h] = value
            span_got[h, g] = value
        for h in range(HL):
            to_span(lambda to: span_pack.at[h], span_got.at[h, g], s3.at[h], r3.at[h])

    def attend(h, seg, last):
        def block(i, _):
            rows = pl.ds(pl.multiple_of(i * BQ, BQ), BQ)
            blocks = pl.ds(pl.multiple_of(i * (BQ // TB), BQ // TB), BQ // TB)
            q = qx[h, blocks].reshape(BQ, 128)
            m = max_ref[h, rows, 0:1]
            acc = acc_ref[h, rows, :]
            for c in range(ROWS // BK):
                k = kx[h, seg, c * BK : (c + 1) * BK, :]
                v = vx[h, seg, c * BK : (c + 1) * BK, :]
                s = lax.dot_general(q, k, (((1,), (1,)), ((), ())), preferred_element_type=F32)
                top = jnp.maximum(m, jnp.max(s, axis=1, keepdims=True))
                w = jnp.exp2(s - top).astype(BF)
                acc = acc * jnp.exp2(m - top) + jnp.dot(w, v, preferred_element_type=F32)
                m = top
            max_ref[h, rows, :] = jnp.broadcast_to(m, (BQ, 128))
            acc_ref[h, rows, :] = acc

            @pl.when(last)
            def _():
                done = acc_ref[h, rows, :]
                gated = (done / swap(done) * gate_row[h]).reshape(BQ // TB, TB, 128)
                mask = low_lanes((BQ // TB, 64, 128))
                out_pack[h, blocks] = jnp.where(mask, gated[:, :64], swap(gated[:, 64:])).astype(BF)

                def send(b, _):
                    to = i * (BQ // TB) + b

                    @pl.when(to != sp)
                    def _():
                        pltpu.make_async_remote_copy(
                            src_ref=out_pack.at[h, to], dst_ref=out_got.at[h, sp],
                            send_sem=os.at[h], recv_sem=orr.at[h],
                            device_id={"sp": to}, device_id_type=MESH,
                        ).start()

                    @pl.when(to == sp)
                    def _():
                        out_got[h, sp] = out_pack[h, sp]

                    return 0

                lax.fori_loop(0, BQ // TB, send, 0)

            return 0

        lax.fori_loop(0, ROWS // BQ, block, 0)

    order = [(0, 0), (1, 0), (2, 0), (0, 1), (0, 2), (1, 1), (1, 2), (2, 2), (2, 1)]

    def step(i, _):
        @pl.when(i < 3)
        def _():
            take_queries(i)

        @pl.when(i == 2)
        def _():
            pick_newest()
            send_kv(1)
            send_kv(2)

        @pl.when(i == 3)
        def _():
            spread_newest()

        h = jnp.int32(0)
        seg = jnp.int32(0)
        for n, (hn, sn) in enumerate(order):
            h = jnp.where(i == n, hn, h)
            seg = jnp.where(i == n, sn, seg)

        @pl.when(seg == 1)
        def _():
            take_own(h)

        @pl.when(seg == 2)
        def _():
            take_newest(h)

        last = jnp.logical_or(i == 4, jnp.logical_or(i == 6, i == 8))
        attend(h, seg, last)
        return 0

    lax.fori_loop(0, len(order), step, 0)

    for h in range(HL):
        wait_bytes(out_got.at[h, pl.ds(0, N - 1)], orr.at[h])
    low = low_lanes((64, 128))
    for t in range(D // 128):
        j = 2 * t
        a = out_got[j % HL, j // HL].astype(F32)
        b = out_got[(j + 1) % HL, (j + 1) // HL].astype(F32)
        cols = slice(t * 128, (t + 1) * 128)
        o_ref[0, 0:64, cols] = jnp.where(low, a, swap(b)).astype(BF)
        o_ref[0, 64:128, cols] = jnp.where(low, swap(a), b).astype(BF)

    wait_bytes(kv8.at[pl.ds(0, N - 1)], s1)
    wait_bytes(part.at[pl.ds(0, N - 1)], s2)
    for h in range(HL):
        wait_bytes(q_pack.at[h, pl.ds(0, N - 1)], qs.at[h])
        wait_bytes(kv_pack.at[h, pl.ds(0, N - 1)], kvs.at[h])
        wait_bytes(span_got.at[h, pl.ds(0, N - 1)], s3.at[h])
        wait_bytes(out_pack.at[h, pl.ds(0, N - 1)], os.at[h])


def per_device(*args):
    any_ = pl.BlockSpec(memory_space=pl.ANY)
    smem = pl.BlockSpec(memory_space=pltpu.SMEM)
    V = pltpu.VMEM
    dma = pltpu.SemaphoreType.DMA
    return pl.pallas_call(
        kernel,
        out_shape=jax.ShapeDtypeStruct((1, TB, D), BF),
        in_specs=[any_] * 6 + [smem] * 3,
        out_specs=pl.BlockSpec(memory_space=pltpu.VMEM),
        scratch_shapes=[
            V((TB, D), BF), V((TB, D), BF), V((TB, D), BF),
            V((ROWS, HL * 64), BF), V((ROWS, HL * 64), BF), V((64, D), F32), V((HL, 1, 128), F32),
            V((HL, N, 64, 128), BF), V((HL, N, TB, 128), BF),
            V((HL, N, 64, 128), BF), V((HL, N, TB, 128), BF),
            V((N, 16, D), BF), V((N, 16, D), BF), V((16, D), BF), V((N, 16, 256), BF),
            V((HL, TB, 128), BF), V((HL, N, TB, 128), BF),
            V((HL, N, TB, 128), BF), V((HL, 3, ROWS, 128), BF), V((HL, 3, ROWS, 128), BF),
            V((HL, ROWS, 128), F32), V((HL, ROWS, 128), F32),
            V((HL, N, 64, 128), BF), V((HL, N, 64, 128), BF),
            dma((6,)), dma((HL,)), dma((HL,)), dma((HL,)), dma((HL,)),
            dma, dma, dma, dma, dma((HL,)), dma((HL,)), dma((HL,)), dma((HL,)),
        ],
        compiler_params=pltpu.CompilerParams(
            collective_id=0, has_side_effects=True, vmem_limit_bytes=60 * 2**20
        ),
        cost_estimate=pl.CostEstimate(
            flops=9 * 2 * 2 * ROWS * ROWS * 64, bytes_accessed=6 * 2**20,
            transcendentals=9 * ROWS * ROWS,
        ),
    )(*args)


def solution(mesh):
    placed = (
        P("span", "sp", None),
        P("span", "sp", None),
        P("span", "sp", None),
        P("span", None, "sp"),
        P("span", None, "sp"),
        P(),
        P("span"),
        P("span"),
        P(),
    )
    return jax.shard_map(
        per_device, mesh=mesh, in_specs=placed, out_specs=P("span", "sp", None), check_vma=False
    )
```

```python
import functools
import math

import jax
import jax.numpy as jnp
from jax import lax
from jax.experimental import pallas as pl
from jax.experimental.pallas import tpu as pltpu
from jax.sharding import PartitionSpec as P

MESH = pl.DeviceIdType.MESH
N = 16
TB = 128
HL = 3
ROWS = 2048
D = 3072
BF = jnp.bfloat16
F32 = jnp.float32
SCALE = 64 ** -0.5 * math.log2(math.e)
BQ = 1024
NEG = -1e30


def swap(x):
    return pltpu.roll(x, 64, x.ndim - 1)


def low_lanes(shape):
    return lax.broadcasted_iota(jnp.int32, shape, len(shape) - 1) < 64


def kernel(
    q_hbm, k_hbm, v_hbm, ck_hbm, cv_hbm, gate_hbm, plen_ref, level_ref, fin_ref, o_ref,
    q_in, k_in, v_in, ck_in, cv_in, gate_in, gate_row,
    q_pack, kv_pack, q_got, kv_got, kv8, near, pick, part, span_pack, span_got,
    qx, kx, vx, acc_ref, max_ref, out_pack, out_got,
    in_sem, qs, qr, kvs, kvr, s1, r1, s2, r2, s3, r3, os, orr,
):
    sp = lax.axis_index("sp")
    g = lax.axis_index("span")
    newest = fin_ref[0]

    def sp_peer(d):
        return lax.rem(sp + d, N)

    def span_peer(d):
        return lax.rem(g + d, N)

    barrier = pltpu.get_barrier_semaphore()

    def greet(d, _):
        pl.semaphore_signal(barrier, inc=1, device_id={"sp": sp_peer(d)}, device_id_type=MESH)
        pl.semaphore_signal(barrier, inc=1, device_id={"span": span_peer(d)}, device_id_type=MESH)
        return 0

    lax.fori_loop(1, N, greet, 0)

    loads = [
        pltpu.make_async_copy(src, dst, in_sem.at[i])
        for i, (src, dst) in enumerate(
            [
                (q_hbm.at[0], q_in),
                (k_hbm.at[0], k_in),
                (v_hbm.at[0], v_in),
                (ck_hbm.at[0], ck_in),
                (cv_hbm.at[0], cv_in),
                (gate_hbm, gate_in),
            ]
        )
    ]
    for load in loads:
        load.start()

    def wait_bytes(ref, sem):
        pltpu.make_async_copy(ref, ref, sem).wait()

    def to_sp(src_of, dst, send, recv):
        def body(d, _):
            to = sp_peer(d)
            pltpu.make_async_remote_copy(
                src_ref=src_of(to), dst_ref=dst, send_sem=send, recv_sem=recv,
                device_id={"sp": to}, device_id_type=MESH,
            ).start()
            return 0

        lax.fori_loop(1, N, body, 0)

    def to_span(src_of, dst, send, recv):
        def body(d, _):
            to = span_peer(d)
            pltpu.make_async_remote_copy(
                src_ref=src_of(to), dst_ref=dst, send_sem=send, recv_sem=recv,
                device_id={"span": to}, device_id_type=MESH,
            ).start()
            return 0

        lax.fori_loop(1, N, body, 0)

    loads[0].wait()
    low = low_lanes((64, 128))
    for t in range(D // 128):
        x = q_in[:, t * 128 : (t + 1) * 128].astype(F32)
        first, second = x[:64], x[64:]
        even = jnp.where(low, first, swap(second)).astype(BF)
        odd = jnp.where(low, swap(first), second).astype(BF)
        for j, value in ((2 * t, even), (2 * t + 1, odd)):
            q_pack[j % HL, j // HL] = value
    for h in range(HL):
        q_got[h, sp] = q_pack[h, sp]
    pl.semaphore_wait(barrier, 2 * (N - 1))
    for h in range(HL):
        to_sp(lambda to: q_pack.at[h, to], q_got.at[h, sp], qs.at[h], qr.at[h])

    loads[1].wait()
    loads[2].wait()
    for t in range(D // 128):
        k = k_in[:, t * 128 : (t + 1) * 128].T
        v = v_in[:, t * 128 : (t + 1) * 128].T
        for j in (2 * t, 2 * t + 1):
            half = slice(64 * (j - 2 * t), 64 * (j - 2 * t + 1))
            kv_pack[j % HL, j // HL, 0:64] = k[half]
            kv_pack[j % HL, j // HL, 64:128] = v[half]
    for h in range(HL):
        kv_got[h, sp] = kv_pack[h, sp]

    def send_kv(h):
        to_sp(lambda to: kv_pack.at[h, to], kv_got.at[h, sp], kvs.at[h], kvr.at[h])

    send_kv(0)

    def eight(i, _):
        rows = pl.ds(pl.multiple_of(i * 16, 16), 16)
        k = k_in[rows, :].astype(F32)
        v = v_in[rows, :].astype(F32)
        kv8[2 * i] = jnp.concatenate([k[:8], v[:8]], axis=0).astype(BF)
        kv8[2 * i + 1] = jnp.concatenate([k[8:], v[8:]], axis=0).astype(BF)
        return 0

    lax.fori_loop(0, N // 2, eight, 0)
    near[g] = kv8[g]
    to_span(lambda to: kv8.at[to], near.at[g], s1, r1)

    loads[5].wait()
    low1 = low_lanes((1, 128))
    for h in range(HL):
        j = sp * HL + h
        tile = pl.ds(pl.multiple_of(lax.div(j, 2) * 128, 128), 128)
        chosen = lax.broadcasted_iota(jnp.int32, (64, 128), 0) == level_ref[0]
        row = jnp.sum(jnp.where(chosen, gate_in[:, tile], 0.0), axis=0, keepdims=True)
        odd = lax.rem(j, 2)
        gate_row[h] = jnp.where(jnp.zeros((1, 128), jnp.int32) + odd == 1, swap(row), row)

    loads[3].wait()
    loads[4].wait()
    def first_key(h):
        return ck_in[64 * h : 64 * h + 64, 0:128].astype(F32)[:, 0:1]

    spare = [jnp.broadcast_to(first_key(h), (64, 128)) for h in range(HL)]

    def cache(i, _):
        lanes = pl.ds(pl.multiple_of(i * 128, 128), 128)
        valid = lax.broadcasted_iota(jnp.int32, (64, 128), 1) + i * 128 < plen_ref[0]
        one = jnp.where(valid, 1.0, 0.0).astype(BF)
        for h in range(HL):
            k = ck_in[64 * h : 64 * h + 64, lanes].astype(F32)
            v = cv_in[64 * h : 64 * h + 64, lanes].astype(F32)
            k = jnp.where(valid, k, spare[h]).astype(BF)
            kx[h, 0, 0:64, lanes] = k
            kx[h, 0, 64:128, lanes] = k
            vx[h, 0, 0:64, lanes] = jnp.where(valid, v, 0.0).astype(BF)
            vx[h, 0, 64:128, lanes] = one
        return 0

    lax.fori_loop(0, ROWS // 128, cache, 0)
    used = jnp.zeros((64, ROWS), jnp.int32) + g > newest
    one = jnp.where(used, 1.0, 0.0).astype(BF)
    for h in range(HL):
        vx[h, 1, 64:128, :] = jnp.ones((64, ROWS), BF)
        vx[h, 2, 64:128, :] = one

    def clear(h, _):
        acc_ref[h] = jnp.zeros((ROWS, 128), F32)
        max_ref[h] = jnp.full((ROWS, 128), NEG, F32)
        return 0

    lax.fori_loop(0, HL, clear, 0)

    def take_queries(h):
        wait_bytes(q_got.at[h, pl.ds(0, N - 1)], qr.at[h])
        mask = low_lanes((64, 128))

        def body(n, _):
            for b in range(4):
                b = n * 4 + b
                x = q_got[h, b].astype(F32) * SCALE
                r = swap(x)
                qx[h, b, 0:64] = jnp.where(mask, x, r - r.astype(BF).astype(F32)).astype(BF)
                qx[h, b, 64:128] = jnp.where(mask, r, x - x.astype(BF).astype(F32)).astype(BF)
            return 0

        lax.fori_loop(0, N // 4, body, 0)

    def take_own(h):
        wait_bytes(kv_got.at[h, pl.ds(0, N - 1)], kvr.at[h])
        for b in range(N):
            lanes = slice(b * TB, (b + 1) * TB)
            k = kv_got[h, b, 0:64]
            kx[h, 1, 0:64, lanes] = k
            kx[h, 1, 64:128, lanes] = k
            vx[h, 1, 0:64, lanes] = kv_got[h, b, 64:128]

    def take_newest(h):
        wait_bytes(span_got.at[h, pl.ds(0, N - 1)], r3.at[h])
        used = jnp.zeros((64, 128), jnp.int32) + g > newest
        spare = jnp.broadcast_to(kx[h, 0, 0:64, 0:128].astype(F32)[:, 0:1], (64, 128))
        for b in range(N):
            lanes = slice(b * TB, (b + 1) * TB)
            k = jnp.where(used, span_got[h, b, 0:64].astype(F32), spare).astype(BF)
            v = jnp.where(used, span_got[h, b, 64:128].astype(F32), 0.0).astype(BF)
            kx[h, 2, 0:64, lanes] = k
            kx[h, 2, 64:128, lanes] = k
            vx[h, 2, 0:64, lanes] = v

    def window(s):
        return pl.ds(pl.multiple_of(lax.div(s * HL, 2) * 128, 128), 256)

    def pick_newest():
        wait_bytes(near.at[pl.ds(0, N - 1)], r1)

        def choose(n, _):
            lanes = pl.ds(pl.multiple_of(n * 512, 512), 512)
            kept = jnp.zeros((16, 512), F32)
            for j in range(N):
                chosen = jnp.zeros((16, 512), jnp.int32) + newest == j
                kept = jnp.where(chosen, near[j, :, lanes].astype(F32), kept)
            pick[:, lanes] = kept.astype(BF)
            return 0

        lax.fori_loop(0, D // 512, choose, 0)
        part[sp] = pick[:, window(sp)]
        to_sp(lambda to: pick.at[:, window(to)], part.at[sp], s2, r2)

    def spread_newest():
        wait_bytes(part.at[pl.ds(0, N - 1)], r2)
        x = part[...].astype(F32)
        k = x[:, :8].reshape(TB, 256)
        v = x[:, 8:].reshape(TB, 256)
        odd = jnp.zeros((TB, 64), jnp.int32) + lax.rem(sp, 2) == 1

        def piece(y, h):
            return jnp.where(odd, y[:, 64 * (h + 1) : 64 * (h + 2)], y[:, 64 * h : 64 * (h + 1)])

        for h in range(HL):
            value = jnp.concatenate([piece(k, h), piece(v, h)], axis=1).T.astype(BF)
            span_pack[h] = value
            span_got[h, g] = value
        for h in range(HL):
            to_span(lambda to: span_pack.at[h], span_got.at[h, g], s3.at[h], r3.at[h])

    def attend(h, seg, last):
        def block(i, _):
            rows = pl.ds(pl.multiple_of(i * BQ, BQ), BQ)
            blocks = pl.ds(pl.multiple_of(i * (BQ // TB), BQ // TB), BQ // TB)
            q = qx[h, blocks].reshape(BQ, 128)
            m = max_ref[h, rows, :]
            acc = acc_ref[h, rows, :]
            s = jnp.dot(q, kx[h, seg], preferred_element_type=F32)
            top = jnp.maximum(m, jnp.broadcast_to(jnp.max(s, axis=1, keepdims=True), (BQ, 128)))
            w = jnp.exp2(s - jnp.tile(top, (1, ROWS // 128))).astype(BF)
            new = lax.dot_general(w, vx[h, seg], (((1,), (1,)), ((), ())), preferred_element_type=F32)
            max_ref[h, rows, :] = top
            acc_ref[h, rows, :] = acc * jnp.exp2(m - top) + new

            @pl.when(last)
            def _():
                done = acc_ref[h, rows, :]
                gated = (done / swap(done) * gate_row[h]).reshape(BQ // TB, TB, 128)
                mask = low_lanes((BQ // TB, 64, 128))
                out_pack[h, blocks] = jnp.where(mask, gated[:, :64], swap(gated[:, 64:])).astype(BF)

                def send(b, _):
                    to = i * (BQ // TB) + b

                    @pl.when(to != sp)
                    def _():
                        pltpu.make_async_remote_copy(
                            src_ref=out_pack.at[h, to], dst_ref=out_got.at[h, sp],
                            send_sem=os.at[h], recv_sem=orr.at[h],
                            device_id={"sp": to}, device_id_type=MESH,
                        ).start()

                    @pl.when(to == sp)
                    def _():
                        out_got[h, sp] = out_pack[h, sp]

                    return 0

                lax.fori_loop(0, BQ // TB, send, 0)

            return 0

        lax.fori_loop(0, ROWS // BQ, block, 0)

    order = [(0, 0), (1, 0), (2, 0), (0, 1), (0, 2), (1, 1), (1, 2), (2, 2), (2, 1)]

    def step(i, _):
        @pl.when(i < 3)
        def _():
            take_queries(i)

        @pl.when(i == 2)
        def _():
            pick_newest()
            send_kv(1)
            send_kv(2)

        @pl.when(i == 3)
        def _():
            spread_newest()

        h = jnp.int32(0)
        seg = jnp.int32(0)
        for n, (hn, sn) in enumerate(order):
            h = jnp.where(i == n, hn, h)
            seg = jnp.where(i == n, sn, seg)

        @pl.when(seg == 1)
        def _():
            take_own(h)

        @pl.when(seg == 2)
        def _():
            take_newest(h)

        last = jnp.logical_or(i == 4, jnp.logical_or(i == 6, i == 8))
        attend(h, seg, last)
        return 0

    lax.fori_loop(0, len(order), step, 0)

    for h in range(HL):
        wait_bytes(out_got.at[h, pl.ds(0, N - 1)], orr.at[h])
    low = low_lanes((64, 128))
    for t in range(D // 128):
        j = 2 * t
        a = out_got[j % HL, j // HL].astype(F32)
        b = out_got[(j + 1) % HL, (j + 1) // HL].astype(F32)
        cols = slice(t * 128, (t + 1) * 128)
        o_ref[0, 0:64, cols] = jnp.where(low, a, swap(b)).astype(BF)
        o_ref[0, 64:128, cols] = jnp.where(low, swap(a), b).astype(BF)

    wait_bytes(kv8.at[pl.ds(0, N - 1)], s1)
    wait_bytes(part.at[pl.ds(0, N - 1)], s2)
    for h in range(HL):
        wait_bytes(q_pack.at[h, pl.ds(0, N - 1)], qs.at[h])
        wait_bytes(kv_pack.at[h, pl.ds(0, N - 1)], kvs.at[h])
        wait_bytes(span_got.at[h, pl.ds(0, N - 1)], s3.at[h])
        wait_bytes(out_pack.at[h, pl.ds(0, N - 1)], os.at[h])


def per_device(queries, keys, values, cache_keys, cache_values, *rest):
    args = (queries, keys, values, cache_keys.swapaxes(1, 2), cache_values.swapaxes(1, 2), *rest)
    any_ = pl.BlockSpec(memory_space=pl.ANY)
    smem = pl.BlockSpec(memory_space=pltpu.SMEM)
    V = pltpu.VMEM
    dma = pltpu.SemaphoreType.DMA
    return pl.pallas_call(
        kernel,
        out_shape=jax.ShapeDtypeStruct((1, TB, D), BF),
        in_specs=[any_] * 6 + [smem] * 3,
        out_specs=pl.BlockSpec(memory_space=pltpu.VMEM),
        scratch_shapes=[
            V((TB, D), BF), V((TB, D), BF), V((TB, D), BF),
            V((HL * 64, ROWS), BF), V((HL * 64, ROWS), BF), V((64, D), F32), V((HL, 1, 128), F32),
            V((HL, N, 64, 128), BF), V((HL, N, TB, 128), BF),
            V((HL, N, 64, 128), BF), V((HL, N, TB, 128), BF),
            V((N, 16, D), BF), V((N, 16, D), BF), V((16, D), BF), V((N, 16, 256), BF),
            V((HL, TB, 128), BF), V((HL, N, TB, 128), BF),
            V((HL, N, TB, 128), BF), V((HL, 3, 128, ROWS), BF), V((HL, 3, 128, ROWS), BF),
            V((HL, ROWS, 128), F32), V((HL, ROWS, 128), F32),
            V((HL, N, 64, 128), BF), V((HL, N, 64, 128), BF),
            dma((6,)), dma((HL,)), dma((HL,)), dma((HL,)), dma((HL,)),
            dma, dma, dma, dma, dma((HL,)), dma((HL,)), dma((HL,)), dma((HL,)),
        ],
        compiler_params=pltpu.CompilerParams(
            collective_id=0, has_side_effects=True, vmem_limit_bytes=60 * 2**20
        ),
        cost_estimate=pl.CostEstimate(
            flops=9 * 2 * 2 * ROWS * ROWS * 64, bytes_accessed=6 * 2**20,
            transcendentals=9 * ROWS * ROWS,
        ),
    )(*args)


def solution(mesh):
    placed = (
        P("span", "sp", None),
        P("span", "sp", None),
        P("span", "sp", None),
        P("span", None, "sp"),
        P("span", None, "sp"),
        P(),
        P("span"),
        P("span"),
        P(),
    )
    return jax.shard_map(
        per_device, mesh=mesh, in_specs=placed, out_specs=P("span", "sp", None), check_vma=False
    )
```

```python
import functools
import math

import jax
import jax.numpy as jnp
from jax import lax
from jax.experimental import pallas as pl
from jax.experimental.pallas import tpu as pltpu
from jax.sharding import PartitionSpec as P

MESH = pl.DeviceIdType.MESH
N = 16
TB = 128
HL = 3
ROWS = 2048
D = 3072
BF = jnp.bfloat16
F32 = jnp.float32
SCALE = 64 ** -0.5 * math.log2(math.e)
BQ = 1024
NEG = -1e30
PICK = 2
SPREAD = 3
FORWARD = {4: (0,), 5: (1, 2)}


def swap(x):
    return pltpu.roll(x, 64, x.ndim - 1)


def low_lanes(shape):
    return lax.broadcasted_iota(jnp.int32, shape, len(shape) - 1) < 64


def kernel(
    q_hbm, k_hbm, v_hbm, ck_hbm, cv_hbm, gate_hbm, plen_ref, level_ref, fin_ref, o_ref,
    q_in, k_in, v_in, ck_in, cv_in, gate_in, gate_row,
    q_pack, kv_pack, q_got, kv_got, kv8, mate, mine, near, pick, part, span_pack, span_got,
    qx, kx, vx, acc_ref, max_ref, out_pack, out_got,
    in_sem, qs, qr, kvs, kvr, s0, r0, s1, r1, s2, r2, s3, r3, s4, r4, os, orr,
):
    sp = lax.axis_index("sp")
    g = lax.axis_index("span")
    newest = fin_ref[0]
    core = lax.rem(g, 2)
    chip = lax.div(g, 2)
    mate_id = {"span": g + 1 - 2 * core}

    def sp_peer(d):
        return lax.rem(sp + d, N)

    def chip_peer(d):
        return lax.rem(chip + d, N // 2)

    barrier = pltpu.get_barrier_semaphore()

    def greet(d, _):
        pl.semaphore_signal(barrier, inc=1, device_id={"sp": sp_peer(d)}, device_id_type=MESH)
        return 0

    lax.fori_loop(1, N, greet, 0)

    def greet_chip(d, _):
        to = {"span": 2 * chip_peer(d) + core}
        pl.semaphore_signal(barrier, inc=1, device_id=to, device_id_type=MESH)
        return 0

    lax.fori_loop(1, N // 2, greet_chip, 0)
    pl.semaphore_signal(barrier, inc=1, device_id=mate_id, device_id_type=MESH)

    loads = [
        pltpu.make_async_copy(src, dst, in_sem.at[i])
        for i, (src, dst) in enumerate(
            [
                (q_hbm.at[0], q_in),
                (k_hbm.at[0], k_in),
                (v_hbm.at[0], v_in),
                (ck_hbm.at[0], ck_in),
                (cv_hbm.at[0], cv_in),
                (gate_hbm, gate_in),
            ]
        )
    ]
    for load in loads:
        load.start()

    def wait_bytes(ref, sem):
        pltpu.make_async_copy(ref, ref, sem).wait()

    def to_sp(src_of, dst, send, recv):
        def body(d, _):
            to = sp_peer(d)
            pltpu.make_async_remote_copy(
                src_ref=src_of(to), dst_ref=dst, send_sem=send, recv_sem=recv,
                device_id={"sp": to}, device_id_type=MESH,
            ).start()
            return 0

        lax.fori_loop(1, N, body, 0)

    def to_chips(src_of, dst, send, recv):
        def body(d, _):
            to = chip_peer(d)
            pltpu.make_async_remote_copy(
                src_ref=src_of(to), dst_ref=dst, send_sem=send, recv_sem=recv,
                device_id={"span": 2 * to + core}, device_id_type=MESH,
            ).start()
            return 0

        lax.fori_loop(1, N // 2, body, 0)

    def to_mate(src, dst, send, recv):
        pltpu.make_async_remote_copy(
            src_ref=src, dst_ref=dst, send_sem=send, recv_sem=recv,
            device_id=mate_id, device_id_type=MESH,
        ).start()

    loads[0].wait()
    low = low_lanes((64, 128))
    for t in range(D // 128):
        x = q_in[:, t * 128 : (t + 1) * 128].astype(F32)
        first, second = x[:64], x[64:]
        even = jnp.where(low, first, swap(second)).astype(BF)
        odd = jnp.where(low, swap(first), second).astype(BF)
        for j, value in ((2 * t, even), (2 * t + 1, odd)):
            q_pack[j % HL, j // HL] = value
    for h in range(HL):
        q_got[h, sp] = q_pack[h, sp]
    pl.semaphore_wait(barrier, N - 1 + N // 2)

    def send_q(h):
        to_sp(lambda to: q_pack.at[h, to], q_got.at[h, sp], qs.at[h], qr.at[h])

    send_q(0)

    loads[1].wait()
    loads[2].wait()

    def eight(i, _):
        rows = pl.ds(pl.multiple_of(i * 16, 16), 16)
        k = k_in[rows, :].astype(F32)
        v = v_in[rows, :].astype(F32)
        kv8[0, i] = jnp.concatenate([k[:8], v[:8]], axis=0).astype(BF)
        kv8[1, i] = jnp.concatenate([k[8:], v[8:]], axis=0).astype(BF)
        return 0

    lax.fori_loop(0, N // 2, eight, 0)
    to_mate(kv8.at[1 - core], mate, s0, r0)
    send_q(1)

    for t in range(D // 128):
        k = k_in[:, t * 128 : (t + 1) * 128].T
        v = v_in[:, t * 128 : (t + 1) * 128].T
        for j in (2 * t, 2 * t + 1):
            half = slice(64 * (j - 2 * t), 64 * (j - 2 * t + 1))
            kv_pack[j % HL, j // HL, 0:64] = k[half]
            kv_pack[j % HL, j // HL, 64:128] = v[half]
    for h in range(HL):
        kv_got[h, sp] = kv_pack[h, sp]

    def send_kv(h):
        to_sp(lambda to: kv_pack.at[h, to], kv_got.at[h, sp], kvs.at[h], kvr.at[h])

    send_q(2)
    send_kv(0)

    wait_bytes(mate, r0)

    def side(i, _):
        other = jnp.zeros((16, D // 2), jnp.int32) + lax.rem(newest, 2) != core
        for half in range(2):
            lanes = slice(half * (D // 2), (half + 1) * (D // 2))
            own = kv8[core, i, :, lanes].astype(F32)
            mine[i, :, lanes] = jnp.where(other, mate[i, :, lanes].astype(F32), own).astype(BF)
        return 0

    lax.fori_loop(0, N // 2, side, 0)
    near[chip] = mine[chip]
    to_chips(lambda to: mine.at[to], near.at[chip], s1, r1)

    loads[5].wait()
    low1 = low_lanes((1, 128))
    for h in range(HL):
        j = sp * HL + h
        tile = pl.ds(pl.multiple_of(lax.div(j, 2) * 128, 128), 128)
        chosen = lax.broadcasted_iota(jnp.int32, (64, 128), 0) == level_ref[0]
        row = jnp.sum(jnp.where(chosen, gate_in[:, tile], 0.0), axis=0, keepdims=True)
        odd = lax.rem(j, 2)
        gate_row[h] = jnp.where(jnp.zeros((1, 128), jnp.int32) + odd == 1, swap(row), row)

    loads[3].wait()
    loads[4].wait()
    def first_key(h):
        return ck_in[64 * h : 64 * h + 64, 0:128].astype(F32)[:, 0:1]

    spare = [jnp.broadcast_to(first_key(h), (64, 128)) for h in range(HL)]

    def cache(i, _):
        lanes = pl.ds(pl.multiple_of(i * 128, 128), 128)
        valid = lax.broadcasted_iota(jnp.int32, (64, 128), 1) + i * 128 < plen_ref[0]
        one = jnp.where(valid, 1.0, 0.0).astype(BF)
        for h in range(HL):
            k = ck_in[64 * h : 64 * h + 64, lanes].astype(F32)
            v = cv_in[64 * h : 64 * h + 64, lanes].astype(F32)
            k = jnp.where(valid, k, spare[h]).astype(BF)
            kx[h, 0, 0:64, lanes] = k
            kx[h, 0, 64:128, lanes] = k
            vx[h, 0, 0:64, lanes] = jnp.where(valid, v, 0.0).astype(BF)
            vx[h, 0, 64:128, lanes] = one
        return 0

    lax.fori_loop(0, ROWS // 128, cache, 0)
    used = jnp.zeros((64, ROWS), jnp.int32) + g > newest
    one = jnp.where(used, 1.0, 0.0).astype(BF)
    for h in range(HL):
        vx[h, 1, 64:128, :] = jnp.ones((64, ROWS), BF)
        vx[h, 2, 64:128, :] = one

    def clear(h, _):
        acc_ref[h] = jnp.zeros((ROWS, 128), F32)
        max_ref[h] = jnp.full((ROWS, 128), NEG, F32)
        return 0

    lax.fori_loop(0, HL, clear, 0)

    def take_queries(h):
        wait_bytes(q_got.at[h, pl.ds(0, N - 1)], qr.at[h])
        mask = low_lanes((64, 128))

        def body(n, _):
            for b in range(4):
                b = n * 4 + b
                x = q_got[h, b].astype(F32) * SCALE
                r = swap(x)
                qx[h, b, 0:64] = jnp.where(mask, x, r - r.astype(BF).astype(F32)).astype(BF)
                qx[h, b, 64:128] = jnp.where(mask, r, x - x.astype(BF).astype(F32)).astype(BF)
            return 0

        lax.fori_loop(0, N // 4, body, 0)

    def take_own(h):
        wait_bytes(kv_got.at[h, pl.ds(0, N - 1)], kvr.at[h])
        for b in range(N):
            lanes = slice(b * TB, (b + 1) * TB)
            k = kv_got[h, b, 0:64]
            kx[h, 1, 0:64, lanes] = k
            kx[h, 1, 64:128, lanes] = k
            vx[h, 1, 0:64, lanes] = kv_got[h, b, 64:128]

    def take_newest(h):
        wait_bytes(span_got.at[h, 0], r4.at[h])
        used = jnp.zeros((64, 128), jnp.int32) + g > newest
        spare = jnp.broadcast_to(kx[h, 0, 0:64, 0:128].astype(F32)[:, 0:1], (64, 128))
        for b in range(N):
            lanes = slice(b * TB, (b + 1) * TB)
            k = jnp.where(used, span_got[h, b % 2, b // 2, 0:64].astype(F32), spare).astype(BF)
            v = jnp.where(used, span_got[h, b % 2, b // 2, 64:128].astype(F32), 0.0).astype(BF)
            kx[h, 2, 0:64, lanes] = k
            kx[h, 2, 64:128, lanes] = k
            vx[h, 2, 0:64, lanes] = v

    def window(s):
        return pl.ds(pl.multiple_of(lax.div(s * HL, 2) * 128, 128), 256)

    def pick_newest():
        wait_bytes(near.at[pl.ds(0, N // 2 - 1)], r1)

        def choose(n, _):
            lanes = pl.ds(pl.multiple_of(n * 512, 512), 512)
            kept = jnp.zeros((16, 512), F32)
            for j in range(N // 2):
                chosen = jnp.zeros((16, 512), jnp.int32) + lax.div(newest, 2) == j
                kept = jnp.where(chosen, near[j, :, lanes].astype(F32), kept)
            pick[:, lanes] = kept.astype(BF)
            return 0

        lax.fori_loop(0, D // 512, choose, 0)
        part[sp] = pick[:, window(sp)]
        to_sp(lambda to: pick.at[:, window(to)], part.at[sp], s2, r2)

    def spread_newest():
        wait_bytes(part.at[pl.ds(0, N - 1)], r2)
        x = part[...].astype(F32)
        k = x[:, :8].reshape(TB, 256)
        v = x[:, 8:].reshape(TB, 256)
        odd = jnp.zeros((TB, 64), jnp.int32) + lax.rem(sp, 2) == 1

        def piece(y, h):
            return jnp.where(odd, y[:, 64 * (h + 1) : 64 * (h + 2)], y[:, 64 * h : 64 * (h + 1)])

        for h in range(HL):
            value = jnp.concatenate([piece(k, h), piece(v, h)], axis=1).T.astype(BF)
            span_pack[h] = value
            span_got[h, core, chip] = value
        for h in range(HL):
            to_chips(lambda to: span_pack.at[h], span_got.at[h, core, chip], s3.at[h], r3.at[h])

    def forward(h):
        wait_bytes(span_got.at[h, core, pl.ds(0, N // 2 - 1)], r3.at[h])
        to_mate(span_got.at[h, core], span_got.at[h, core], s4.at[h], r4.at[h])

    def attend(h, seg, last):
        def block(i, _):
            rows = pl.ds(pl.multiple_of(i * BQ, BQ), BQ)
            blocks = pl.ds(pl.multiple_of(i * (BQ // TB), BQ // TB), BQ // TB)
            q = qx[h, blocks].reshape(BQ, 128)
            m = max_ref[h, rows, :]
            acc = acc_ref[h, rows, :]
            s = jnp.dot(q, kx[h, seg], preferred_element_type=F32)
            top = jnp.maximum(m, jnp.broadcast_to(jnp.max(s, axis=1, keepdims=True), (BQ, 128)))
            w = jnp.exp2(s - jnp.tile(top, (1, ROWS // 128))).astype(BF)
            new = lax.dot_general(w, vx[h, seg], (((1,), (1,)), ((), ())), preferred_element_type=F32)
            max_ref[h, rows, :] = top
            acc_ref[h, rows, :] = acc * jnp.exp2(m - top) + new

            @pl.when(last)
            def _():
                done = acc_ref[h, rows, :]
                gated = (done / swap(done) * gate_row[h]).reshape(BQ // TB, TB, 128)
                mask = low_lanes((BQ // TB, 64, 128))
                out_pack[h, blocks] = jnp.where(mask, gated[:, :64], swap(gated[:, 64:])).astype(BF)

                def send(b, _):
                    to = i * (BQ // TB) + b

                    @pl.when(to != sp)
                    def _():
                        pltpu.make_async_remote_copy(
                            src_ref=out_pack.at[h, to], dst_ref=out_got.at[h, sp],
                            send_sem=os.at[h], recv_sem=orr.at[h],
                            device_id={"sp": to}, device_id_type=MESH,
                        ).start()

                    @pl.when(to == sp)
                    def _():
                        out_got[h, sp] = out_pack[h, sp]

                    return 0

                lax.fori_loop(0, BQ // TB, send, 0)

            return 0

        lax.fori_loop(0, ROWS // BQ, block, 0)

    order = [(0, 0), (1, 0), (2, 0), (0, 1), (1, 1), (0, 2), (1, 2), (2, 2), (2, 1)]

    def step(i, _):
        @pl.when(i < 3)
        def _():
            take_queries(i)

        @pl.when(i == 1)
        def _():
            send_kv(1)

        @pl.when(i == PICK)
        def _():
            pick_newest()

        @pl.when(i == 3)
        def _():
            send_kv(2)

        @pl.when(i == SPREAD)
        def _():
            spread_newest()

        for n, heads in FORWARD.items():
            @pl.when(i == n)
            def _():
                for h in heads:
                    forward(h)

        h = jnp.int32(0)
        seg = jnp.int32(0)
        for n, (hn, sn) in enumerate(order):
            h = jnp.where(i == n, hn, h)
            seg = jnp.where(i == n, sn, seg)

        @pl.when(seg == 1)
        def _():
            take_own(h)

        @pl.when(seg == 2)
        def _():
            take_newest(h)

        last = jnp.logical_or(i == 5, jnp.logical_or(i == 6, i == 8))
        attend(h, seg, last)
        return 0

    lax.fori_loop(0, len(order), step, 0)

    for h in range(HL):
        wait_bytes(out_got.at[h, pl.ds(0, N - 1)], orr.at[h])
    low = low_lanes((64, 128))
    for t in range(D // 128):
        j = 2 * t
        a = out_got[j % HL, j // HL].astype(F32)
        b = out_got[(j + 1) % HL, (j + 1) // HL].astype(F32)
        cols = slice(t * 128, (t + 1) * 128)
        o_ref[0, 0:64, cols] = jnp.where(low, a, swap(b)).astype(BF)
        o_ref[0, 64:128, cols] = jnp.where(low, swap(a), b).astype(BF)

    wait_bytes(mate, s0)
    wait_bytes(mine.at[pl.ds(0, N // 2 - 1)], s1)
    wait_bytes(part.at[pl.ds(0, N - 1)], s2)
    for h in range(HL):
        wait_bytes(q_pack.at[h, pl.ds(0, N - 1)], qs.at[h])
        wait_bytes(kv_pack.at[h, pl.ds(0, N - 1)], kvs.at[h])
        wait_bytes(span_got.at[h, 0, pl.ds(0, N // 2 - 1)], s3.at[h])
        wait_bytes(span_got.at[h, 0], s4.at[h])
        wait_bytes(out_pack.at[h, pl.ds(0, N - 1)], os.at[h])


def per_device(queries, keys, values, cache_keys, cache_values, *rest):
    args = (queries, keys, values, cache_keys.swapaxes(1, 2), cache_values.swapaxes(1, 2), *rest)
    any_ = pl.BlockSpec(memory_space=pl.ANY)
    smem = pl.BlockSpec(memory_space=pltpu.SMEM)
    V = pltpu.VMEM
    dma = pltpu.SemaphoreType.DMA
    return pl.pallas_call(
        kernel,
        out_shape=jax.ShapeDtypeStruct((1, TB, D), BF),
        in_specs=[any_] * 6 + [smem] * 3,
        out_specs=pl.BlockSpec(memory_space=pltpu.VMEM),
        scratch_shapes=[
            V((TB, D), BF), V((TB, D), BF), V((TB, D), BF),
            V((HL * 64, ROWS), BF), V((HL * 64, ROWS), BF), V((64, D), F32), V((HL, 1, 128), F32),
            V((HL, N, 64, 128), BF), V((HL, N, TB, 128), BF),
            V((HL, N, 64, 128), BF), V((HL, N, TB, 128), BF),
            V((2, N // 2, 16, D), BF), V((N // 2, 16, D), BF), V((N // 2, 16, D), BF),
            V((N // 2, 16, D), BF), V((16, D), BF), V((N, 16, 256), BF),
            V((HL, TB, 128), BF), V((HL, 2, N // 2, TB, 128), BF),
            V((HL, N, TB, 128), BF), V((HL, 3, 128, ROWS), BF), V((HL, 3, 128, ROWS), BF),
            V((HL, ROWS, 128), F32), V((HL, ROWS, 128), F32),
            V((HL, N, 64, 128), BF), V((HL, N, 64, 128), BF),
            dma((6,)), dma((HL,)), dma((HL,)), dma((HL,)), dma((HL,)),
            dma, dma, dma, dma, dma, dma, dma((HL,)), dma((HL,)), dma((HL,)), dma((HL,)), dma((HL,)), dma((HL,)),
        ],
        compiler_params=pltpu.CompilerParams(
            collective_id=0, has_side_effects=True, vmem_limit_bytes=60 * 2**20
        ),
        cost_estimate=pl.CostEstimate(
            flops=9 * 2 * 2 * ROWS * ROWS * 64, bytes_accessed=6 * 2**20,
            transcendentals=9 * ROWS * ROWS,
        ),
    )(*args)


def solution(mesh):
    placed = (
        P("span", "sp", None),
        P("span", "sp", None),
        P("span", "sp", None),
        P("span", None, "sp"),
        P("span", None, "sp"),
        P(),
        P("span"),
        P("span"),
        P(),
    )
    return jax.shard_map(
        per_device, mesh=mesh, in_specs=placed, out_specs=P("span", "sp", None), check_vma=False
    )
```

```python
import functools
import math

import jax
import jax.numpy as jnp
from jax import lax
from jax.experimental import pallas as pl
from jax.experimental.pallas import tpu as pltpu
from jax.sharding import PartitionSpec as P

MESH = pl.DeviceIdType.MESH
N = 16
TB = 128
HL = 3
ROWS = 2048
D = 3072
BF = jnp.bfloat16
F32 = jnp.float32
SCALE = 64 ** -0.5 * math.log2(math.e)
BQ = 1024
NEG = -1e30
PICK = 2
SPREAD = 3
FORWARD = {4: (0,), 5: (1,), 6: (2,)}


def swap(x):
    return pltpu.roll(x, 64, x.ndim - 1)


def low_lanes(shape):
    return lax.broadcasted_iota(jnp.int32, shape, len(shape) - 1) < 64


def kernel(
    q_hbm, k_hbm, v_hbm, ck_hbm, cv_hbm, gate_hbm, plen_ref, level_ref, fin_ref, o_ref,
    q_in, k_in, v_in, ck_in, cv_in, gate_in, gate_row,
    q_pack, kv_pack, q_got, kv_got, kv8, mate, mine, near, pick, part, span_pack, span_got,
    qx, kx, vx, acc_ref, max_ref, out_pack, out_got,
    in_sem, qs, qr, kvs, kvr, s0, r0, s1, r1, s2, r2, s3, r3, s4, r4, os, orr,
):
    sp = lax.axis_index("sp")
    g = lax.axis_index("span")
    newest = fin_ref[0]
    core = lax.rem(g, 2)
    chip = lax.div(g, 2)
    mate_id = {"span": g + 1 - 2 * core}

    def sp_peer(d):
        return lax.rem(sp + d, N)

    def chip_peer(d):
        return lax.rem(chip + d, N // 2)

    barrier = pltpu.get_barrier_semaphore()

    def greet(d, _):
        pl.semaphore_signal(barrier, inc=1, device_id={"sp": sp_peer(d)}, device_id_type=MESH)
        return 0

    lax.fori_loop(1, N, greet, 0)

    def greet_chip(d, _):
        to = {"span": 2 * chip_peer(d) + core}
        pl.semaphore_signal(barrier, inc=1, device_id=to, device_id_type=MESH)
        return 0

    lax.fori_loop(1, N // 2, greet_chip, 0)
    pl.semaphore_signal(barrier, inc=1, device_id=mate_id, device_id_type=MESH)

    loads = [
        pltpu.make_async_copy(src, dst, in_sem.at[i])
        for i, (src, dst) in enumerate(
            [
                (q_hbm.at[0], q_in),
                (k_hbm.at[0], k_in),
                (v_hbm.at[0], v_in),
                (ck_hbm.at[0], ck_in),
                (cv_hbm.at[0], cv_in),
                (gate_hbm, gate_in),
            ]
        )
    ]
    for load in loads:
        load.start()

    def wait_bytes(ref, sem):
        pltpu.make_async_copy(ref, ref, sem).wait()

    def to_sp(src_of, dst, send, recv):
        def body(d, _):
            to = sp_peer(d)
            pltpu.make_async_remote_copy(
                src_ref=src_of(to), dst_ref=dst, send_sem=send, recv_sem=recv,
                device_id={"sp": to}, device_id_type=MESH,
            ).start()
            return 0

        lax.fori_loop(1, N, body, 0)

    def to_chips(src_of, dst, send, recv):
        def body(d, _):
            to = chip_peer(d)
            pltpu.make_async_remote_copy(
                src_ref=src_of(to), dst_ref=dst, send_sem=send, recv_sem=recv,
                device_id={"span": 2 * to + core}, device_id_type=MESH,
            ).start()
            return 0

        lax.fori_loop(1, N // 2, body, 0)

    def to_mate(src, dst, send, recv):
        pltpu.make_async_remote_copy(
            src_ref=src, dst_ref=dst, send_sem=send, recv_sem=recv,
            device_id=mate_id, device_id_type=MESH,
        ).start()

    loads[0].wait()
    low = low_lanes((64, 128))
    for t in range(D // 128):
        x = q_in[:, t * 128 : (t + 1) * 128].astype(F32)
        first, second = x[:64], x[64:]
        even = jnp.where(low, first, swap(second)).astype(BF)
        odd = jnp.where(low, swap(first), second).astype(BF)
        for j, value in ((2 * t, even), (2 * t + 1, odd)):
            q_pack[j % HL, j // HL] = value
    for h in range(HL):
        q_got[h, sp] = q_pack[h, sp]
    pl.semaphore_wait(barrier, N - 1 + N // 2)

    def send_q(h):
        to_sp(lambda to: q_pack.at[h, to], q_got.at[h, sp], qs.at[h], qr.at[h])

    send_q(0)

    loads[1].wait()
    loads[2].wait()

    def eight(i, _):
        rows = pl.ds(pl.multiple_of(i * 16, 16), 16)
        k = k_in[rows, :].astype(F32)
        v = v_in[rows, :].astype(F32)
        kv8[0, i] = jnp.concatenate([k[:8], v[:8]], axis=0).astype(BF)
        kv8[1, i] = jnp.concatenate([k[8:], v[8:]], axis=0).astype(BF)
        return 0

    lax.fori_loop(0, N // 2, eight, 0)
    to_mate(kv8.at[1 - core], mate, s0, r0)

    for t in range(D // 128):
        k = k_in[:, t * 128 : (t + 1) * 128].T
        v = v_in[:, t * 128 : (t + 1) * 128].T
        for j in (2 * t, 2 * t + 1):
            half = slice(64 * (j - 2 * t), 64 * (j - 2 * t + 1))
            kv_pack[j % HL, j // HL, 0:64] = k[half]
            kv_pack[j % HL, j // HL, 64:128] = v[half]
    for h in range(HL):
        kv_got[h, sp] = kv_pack[h, sp]

    def send_kv(h):
        to_sp(lambda to: kv_pack.at[h, to], kv_got.at[h, sp], kvs.at[h], kvr.at[h])

    send_kv(0)
    send_q(1)
    send_q(2)

    wait_bytes(mate, r0)

    def side(i, _):
        other = jnp.zeros((16, D // 2), jnp.int32) + lax.rem(newest, 2) != core
        for half in range(2):
            lanes = slice(half * (D // 2), (half + 1) * (D // 2))
            own = kv8[core, i, :, lanes].astype(F32)
            mine[i, :, lanes] = jnp.where(other, mate[i, :, lanes].astype(F32), own).astype(BF)
        return 0

    lax.fori_loop(0, N // 2, side, 0)
    near[chip] = mine[chip]
    to_chips(lambda to: mine.at[to], near.at[chip], s1, r1)

    loads[5].wait()
    low1 = low_lanes((1, 128))
    for h in range(HL):
        j = sp * HL + h
        tile = pl.ds(pl.multiple_of(lax.div(j, 2) * 128, 128), 128)
        chosen = lax.broadcasted_iota(jnp.int32, (64, 128), 0) == level_ref[0]
        row = jnp.sum(jnp.where(chosen, gate_in[:, tile], 0.0), axis=0, keepdims=True)
        odd = lax.rem(j, 2)
        gate_row[h] = jnp.where(jnp.zeros((1, 128), jnp.int32) + odd == 1, swap(row), row)

    loads[3].wait()
    loads[4].wait()
    def first_key(h):
        return ck_in[64 * h : 64 * h + 64, 0:128].astype(F32)[:, 0:1]

    spare = [jnp.broadcast_to(first_key(h), (64, 128)) for h in range(HL)]

    def cache(i, _):
        lanes = pl.ds(pl.multiple_of(i * 128, 128), 128)
        valid = lax.broadcasted_iota(jnp.int32, (64, 128), 1) + i * 128 < plen_ref[0]
        one = jnp.where(valid, 1.0, 0.0).astype(BF)
        for h in range(HL):
            k = ck_in[64 * h : 64 * h + 64, lanes].astype(F32)
            v = cv_in[64 * h : 64 * h + 64, lanes].astype(F32)
            k = jnp.where(valid, k, spare[h]).astype(BF)
            kx[h, 0, 0:64, lanes] = k
            kx[h, 0, 64:128, lanes] = k
            vx[h, 0, 0:64, lanes] = jnp.where(valid, v, 0.0).astype(BF)
            vx[h, 0, 64:128, lanes] = one
        return 0

    lax.fori_loop(0, ROWS // 128, cache, 0)
    used = jnp.zeros((64, ROWS), jnp.int32) + g > newest
    one = jnp.where(used, 1.0, 0.0).astype(BF)
    for h in range(HL):
        vx[h, 1, 64:128, :] = jnp.ones((64, ROWS), BF)
        vx[h, 2, 64:128, :] = one

    def clear(h, _):
        acc_ref[h] = jnp.zeros((ROWS, 128), F32)
        max_ref[h] = jnp.full((ROWS, 128), NEG, F32)
        return 0

    lax.fori_loop(0, HL, clear, 0)

    def take_queries(h):
        wait_bytes(q_got.at[h, pl.ds(0, N - 1)], qr.at[h])
        mask = low_lanes((64, 128))

        def body(n, _):
            for b in range(4):
                b = n * 4 + b
                x = q_got[h, b].astype(F32) * SCALE
                r = swap(x)
                qx[h, b, 0:64] = jnp.where(mask, x, r - r.astype(BF).astype(F32)).astype(BF)
                qx[h, b, 64:128] = jnp.where(mask, r, x - x.astype(BF).astype(F32)).astype(BF)
            return 0

        lax.fori_loop(0, N // 4, body, 0)

    def take_own(h):
        wait_bytes(kv_got.at[h, pl.ds(0, N - 1)], kvr.at[h])
        for b in range(N):
            lanes = slice(b * TB, (b + 1) * TB)
            k = kv_got[h, b, 0:64]
            kx[h, 1, 0:64, lanes] = k
            kx[h, 1, 64:128, lanes] = k
            vx[h, 1, 0:64, lanes] = kv_got[h, b, 64:128]

    def take_newest(h):
        wait_bytes(span_got.at[h, 0], r4.at[h])
        used = jnp.zeros((64, 128), jnp.int32) + g > newest
        spare = jnp.broadcast_to(kx[h, 0, 0:64, 0:128].astype(F32)[:, 0:1], (64, 128))
        for b in range(N):
            lanes = slice(b * TB, (b + 1) * TB)
            k = jnp.where(used, span_got[h, b % 2, b // 2, 0:64].astype(F32), spare).astype(BF)
            v = jnp.where(used, span_got[h, b % 2, b // 2, 64:128].astype(F32), 0.0).astype(BF)
            kx[h, 2, 0:64, lanes] = k
            kx[h, 2, 64:128, lanes] = k
            vx[h, 2, 0:64, lanes] = v

    def window(s):
        return pl.ds(pl.multiple_of(lax.div(s * HL, 2) * 128, 128), 256)

    def pick_newest():
        wait_bytes(near.at[pl.ds(0, N // 2 - 1)], r1)

        def choose(n, _):
            lanes = pl.ds(pl.multiple_of(n * 512, 512), 512)
            kept = jnp.zeros((16, 512), F32)
            for j in range(N // 2):
                chosen = jnp.zeros((16, 512), jnp.int32) + lax.div(newest, 2) == j
                kept = jnp.where(chosen, near[j, :, lanes].astype(F32), kept)
            pick[:, lanes] = kept.astype(BF)
            return 0

        lax.fori_loop(0, D // 512, choose, 0)
        part[sp] = pick[:, window(sp)]
        to_sp(lambda to: pick.at[:, window(to)], part.at[sp], s2, r2)

    def spread_newest():
        wait_bytes(part.at[pl.ds(0, N - 1)], r2)
        x = part[...].astype(F32)
        k = x[:, :8].reshape(TB, 256)
        v = x[:, 8:].reshape(TB, 256)
        odd = jnp.zeros((TB, 64), jnp.int32) + lax.rem(sp, 2) == 1

        def piece(y, h):
            return jnp.where(odd, y[:, 64 * (h + 1) : 64 * (h + 2)], y[:, 64 * h : 64 * (h + 1)])

        for h in range(HL):
            value = jnp.concatenate([piece(k, h), piece(v, h)], axis=1).T.astype(BF)
            span_pack[h] = value
            span_got[h, core, chip] = value
        for h in range(HL):
            to_chips(lambda to: span_pack.at[h], span_got.at[h, core, chip], s3.at[h], r3.at[h])

    def forward(h):
        wait_bytes(span_got.at[h, core, pl.ds(0, N // 2 - 1)], r3.at[h])
        to_mate(span_got.at[h, core], span_got.at[h, core], s4.at[h], r4.at[h])

    def attend(h, seg, last):
        def block(i, _):
            rows = pl.ds(pl.multiple_of(i * BQ, BQ), BQ)
            blocks = pl.ds(pl.multiple_of(i * (BQ // TB), BQ // TB), BQ // TB)
            q = qx[h, blocks].reshape(BQ, 128)
            m = max_ref[h, rows, :]
            acc = acc_ref[h, rows, :]
            s = jnp.dot(q, kx[h, seg], preferred_element_type=F32)
            top = jnp.maximum(m, jnp.broadcast_to(jnp.max(s, axis=1, keepdims=True), (BQ, 128)))
            w = jnp.exp2(s - jnp.tile(top, (1, ROWS // 128))).astype(BF)
            new = lax.dot_general(w, vx[h, seg], (((1,), (1,)), ((), ())), preferred_element_type=F32)
            max_ref[h, rows, :] = top
            acc_ref[h, rows, :] = acc * jnp.exp2(m - top) + new

            @pl.when(last)
            def _():
                done = acc_ref[h, rows, :]
                gated = (done / swap(done) * gate_row[h]).reshape(BQ // TB, TB, 128)
                mask = low_lanes((BQ // TB, 64, 128))
                out_pack[h, blocks] = jnp.where(mask, gated[:, :64], swap(gated[:, 64:])).astype(BF)

                def send(b, _):
                    to = i * (BQ // TB) + b

                    @pl.when(to != sp)
                    def _():
                        pltpu.make_async_remote_copy(
                            src_ref=out_pack.at[h, to], dst_ref=out_got.at[h, sp],
                            send_sem=os.at[h], recv_sem=orr.at[h],
                            device_id={"sp": to}, device_id_type=MESH,
                        ).start()

                    @pl.when(to == sp)
                    def _():
                        out_got[h, sp] = out_pack[h, sp]

                    return 0

                lax.fori_loop(0, BQ // TB, send, 0)

            return 0

        lax.fori_loop(0, ROWS // BQ, block, 0)

    order = [(0, 0), (0, 1), (1, 0), (2, 0), (0, 2), (1, 1), (1, 2), (2, 2), (2, 1)]

    def step(i, _):
        @pl.when(i == PICK)
        def _():
            pick_newest()
            send_kv(1)

        @pl.when(i == SPREAD)
        def _():
            spread_newest()
            send_kv(2)

        for n, heads in FORWARD.items():
            @pl.when(i == n)
            def _():
                for h in heads:
                    forward(h)

        h = jnp.int32(0)
        seg = jnp.int32(0)
        for n, (hn, sn) in enumerate(order):
            h = jnp.where(i == n, hn, h)
            seg = jnp.where(i == n, sn, seg)

        @pl.when(seg == 0)
        def _():
            take_queries(h)

        @pl.when(seg == 1)
        def _():
            take_own(h)

        @pl.when(seg == 2)
        def _():
            take_newest(h)

        last = jnp.logical_or(i == 4, jnp.logical_or(i == 6, i == 8))
        attend(h, seg, last)
        return 0

    lax.fori_loop(0, len(order), step, 0)

    for h in range(HL):
        wait_bytes(out_got.at[h, pl.ds(0, N - 1)], orr.at[h])
    low = low_lanes((64, 128))
    for t in range(D // 128):
        j = 2 * t
        a = out_got[j % HL, j // HL].astype(F32)
        b = out_got[(j + 1) % HL, (j + 1) // HL].astype(F32)
        cols = slice(t * 128, (t + 1) * 128)
        o_ref[0, 0:64, cols] = jnp.where(low, a, swap(b)).astype(BF)
        o_ref[0, 64:128, cols] = jnp.where(low, swap(a), b).astype(BF)

    wait_bytes(mate, s0)
    wait_bytes(mine.at[pl.ds(0, N // 2 - 1)], s1)
    wait_bytes(part.at[pl.ds(0, N - 1)], s2)
    for h in range(HL):
        wait_bytes(q_pack.at[h, pl.ds(0, N - 1)], qs.at[h])
        wait_bytes(kv_pack.at[h, pl.ds(0, N - 1)], kvs.at[h])
        wait_bytes(span_got.at[h, 0, pl.ds(0, N // 2 - 1)], s3.at[h])
        wait_bytes(span_got.at[h, 0], s4.at[h])
        wait_bytes(out_pack.at[h, pl.ds(0, N - 1)], os.at[h])


def per_device(queries, keys, values, cache_keys, cache_values, *rest):
    args = (queries, keys, values, cache_keys.swapaxes(1, 2), cache_values.swapaxes(1, 2), *rest)
    any_ = pl.BlockSpec(memory_space=pl.ANY)
    smem = pl.BlockSpec(memory_space=pltpu.SMEM)
    V = pltpu.VMEM
    dma = pltpu.SemaphoreType.DMA
    return pl.pallas_call(
        kernel,
        out_shape=jax.ShapeDtypeStruct((1, TB, D), BF),
        in_specs=[any_] * 6 + [smem] * 3,
        out_specs=pl.BlockSpec(memory_space=pltpu.VMEM),
        scratch_shapes=[
            V((TB, D), BF), V((TB, D), BF), V((TB, D), BF),
            V((HL * 64, ROWS), BF), V((HL * 64, ROWS), BF), V((64, D), F32), V((HL, 1, 128), F32),
            V((HL, N, 64, 128), BF), V((HL, N, TB, 128), BF),
            V((HL, N, 64, 128), BF), V((HL, N, TB, 128), BF),
            V((2, N // 2, 16, D), BF), V((N // 2, 16, D), BF), V((N // 2, 16, D), BF),
            V((N // 2, 16, D), BF), V((16, D), BF), V((N, 16, 256), BF),
            V((HL, TB, 128), BF), V((HL, 2, N // 2, TB, 128), BF),
            V((HL, N, TB, 128), BF), V((HL, 3, 128, ROWS), BF), V((HL, 3, 128, ROWS), BF),
            V((HL, ROWS, 128), F32), V((HL, ROWS, 128), F32),
            V((HL, N, 64, 128), BF), V((HL, N, 64, 128), BF),
            dma((6,)), dma((HL,)), dma((HL,)), dma((HL,)), dma((HL,)),
            dma, dma, dma, dma, dma, dma, dma((HL,)), dma((HL,)), dma((HL,)), dma((HL,)), dma((HL,)), dma((HL,)),
        ],
        compiler_params=pltpu.CompilerParams(
            collective_id=0, has_side_effects=True, vmem_limit_bytes=60 * 2**20
        ),
        cost_estimate=pl.CostEstimate(
            flops=9 * 2 * 2 * ROWS * ROWS * 64, bytes_accessed=6 * 2**20,
            transcendentals=9 * ROWS * ROWS,
        ),
    )(*args)


def solution(mesh):
    placed = (
        P("span", "sp", None),
        P("span", "sp", None),
        P("span", "sp", None),
        P("span", None, "sp"),
        P("span", None, "sp"),
        P(),
        P("span"),
        P("span"),
        P(),
    )
    return jax.shard_map(
        per_device, mesh=mesh, in_specs=placed, out_specs=P("span", "sp", None), check_vma=False
    )
```

```python
import functools
import math

import jax
import jax.numpy as jnp
from jax import lax
from jax.experimental import pallas as pl
from jax.experimental.pallas import tpu as pltpu
from jax.sharding import PartitionSpec as P

MESH = pl.DeviceIdType.MESH
N = 16
TB = 128
HL = 3
ROWS = 2048
D = 3072
BF = jnp.bfloat16
F32 = jnp.float32
SCALE = 64 ** -0.5 * math.log2(math.e)
BQ = 1024
NEG = -1e30
PICK = 2
SPREAD = 3
FORWARD = {4: (0,), 5: (1,), 6: (2,)}


def swap(x):
    return pltpu.roll(x, 64, x.ndim - 1)


def low_lanes(shape):
    return lax.broadcasted_iota(jnp.int32, shape, len(shape) - 1) < 64


def kernel(
    q_hbm, k_hbm, v_hbm, ck_hbm, cv_hbm, gate_hbm, plen_ref, level_ref, fin_ref, o_ref,
    q_in, k_in, v_in, ck_in, cv_in, gate_in, gate_row,
    q_pack, kv_pack, q_got, kv_got, kv8, mate, mine, near, pick, part, span_pack, span_got,
    qx, kx, vx, acc_ref, max_ref, out_pack, out_got,
    in_sem, qs, qr, kvs, kvr, s0, r0, s1, r1, s2, r2, s3, r3, s4, r4, os, orr,
):
    sp = lax.axis_index("sp")
    g = lax.axis_index("span")
    newest = fin_ref[0]
    core = lax.rem(g, 2)
    chip = lax.div(g, 2)
    mate_id = {"span": g + 1 - 2 * core}

    def sp_peer(d):
        return lax.rem(sp + d, N)

    def chip_peer(d):
        return lax.rem(chip + d, N // 2)

    barrier = pltpu.get_barrier_semaphore()

    def greet(d, _):
        pl.semaphore_signal(barrier, inc=1, device_id={"sp": sp_peer(d)}, device_id_type=MESH)
        return 0

    lax.fori_loop(1, N, greet, 0)

    def greet_chip(d, _):
        to = {"span": 2 * chip_peer(d) + core}
        pl.semaphore_signal(barrier, inc=1, device_id=to, device_id_type=MESH)
        return 0

    lax.fori_loop(1, N // 2, greet_chip, 0)
    pl.semaphore_signal(barrier, inc=1, device_id=mate_id, device_id_type=MESH)

    loads = [
        pltpu.make_async_copy(src, dst, in_sem.at[i])
        for i, (src, dst) in enumerate(
            [
                (q_hbm.at[0], q_in),
                (k_hbm.at[0], k_in),
                (v_hbm.at[0], v_in),
                (ck_hbm.at[0], ck_in),
                (cv_hbm.at[0], cv_in),
                (gate_hbm, gate_in),
            ]
        )
    ]
    for load in loads:
        load.start()

    def wait_bytes(ref, sem):
        pltpu.make_async_copy(ref, ref, sem).wait()

    def to_sp(src_of, dst, send, recv):
        def body(d, _):
            to = sp_peer(d)
            pltpu.make_async_remote_copy(
                src_ref=src_of(to), dst_ref=dst, send_sem=send, recv_sem=recv,
                device_id={"sp": to}, device_id_type=MESH,
            ).start()
            return 0

        lax.fori_loop(1, N, body, 0)

    def to_chips(src_of, dst, send, recv):
        def body(d, _):
            to = chip_peer(d)
            pltpu.make_async_remote_copy(
                src_ref=src_of(to), dst_ref=dst, send_sem=send, recv_sem=recv,
                device_id={"span": 2 * to + core}, device_id_type=MESH,
            ).start()
            return 0

        lax.fori_loop(1, N // 2, body, 0)

    def to_mate(src, dst, send, recv):
        pltpu.make_async_remote_copy(
            src_ref=src, dst_ref=dst, send_sem=send, recv_sem=recv,
            device_id=mate_id, device_id_type=MESH,
        ).start()

    loads[0].wait()
    low = low_lanes((64, 128))
    for t in range(D // 128):
        x = q_in[:, t * 128 : (t + 1) * 128].astype(F32)
        first, second = x[:64], x[64:]
        even = jnp.where(low, first, swap(second)).astype(BF)
        odd = jnp.where(low, swap(first), second).astype(BF)
        for j, value in ((2 * t, even), (2 * t + 1, odd)):
            q_pack[j % HL, j // HL] = value
    for h in range(HL):
        q_got[h, sp] = q_pack[h, sp]
    pl.semaphore_wait(barrier, N - 1 + N // 2)

    def send_q(h):
        to_sp(lambda to: q_pack.at[h, to], q_got.at[h, sp], qs.at[h], qr.at[h])

    send_q(0)

    loads[1].wait()
    loads[2].wait()

    def eight(i, _):
        rows = pl.ds(pl.multiple_of(i * 16, 16), 16)
        k = k_in[rows, :].astype(F32)
        v = v_in[rows, :].astype(F32)
        kv8[0, i] = jnp.concatenate([k[:8], v[:8]], axis=0).astype(BF)
        kv8[1, i] = jnp.concatenate([k[8:], v[8:]], axis=0).astype(BF)
        return 0

    lax.fori_loop(0, N // 2, eight, 0)
    to_mate(kv8.at[1 - core], mate, s0, r0)

    for t in range(D // 128):
        k = k_in[:, t * 128 : (t + 1) * 128].T
        v = v_in[:, t * 128 : (t + 1) * 128].T
        for j in (2 * t, 2 * t + 1):
            half = slice(64 * (j - 2 * t), 64 * (j - 2 * t + 1))
            kv_pack[j % HL, j // HL, 0:64] = k[half]
            kv_pack[j % HL, j // HL, 64:128] = v[half]
    for h in range(HL):
        kv_got[h, sp] = kv_pack[h, sp]

    def send_kv(h):
        to_sp(lambda to: kv_pack.at[h, to], kv_got.at[h, sp], kvs.at[h], kvr.at[h])

    send_kv(0)
    send_q(1)
    send_q(2)

    wait_bytes(mate, r0)

    def side(i, _):
        other = jnp.zeros((16, D // 2), jnp.int32) + lax.rem(newest, 2) != core
        for half in range(2):
            lanes = slice(half * (D // 2), (half + 1) * (D // 2))
            own = kv8[core, i, :, lanes].astype(F32)
            mine[i, :, lanes] = jnp.where(other, mate[i, :, lanes].astype(F32), own).astype(BF)
        return 0

    lax.fori_loop(0, N // 2, side, 0)
    near[chip] = mine[chip]
    to_chips(lambda to: mine.at[to], near.at[chip], s1, r1)

    loads[5].wait()
    low1 = low_lanes((1, 128))
    for h in range(HL):
        j = sp * HL + h
        tile = pl.ds(pl.multiple_of(lax.div(j, 2) * 128, 128), 128)
        chosen = lax.broadcasted_iota(jnp.int32, (64, 128), 0) == level_ref[0]
        row = jnp.sum(jnp.where(chosen, gate_in[:, tile], 0.0), axis=0, keepdims=True)
        odd = lax.rem(j, 2)
        gate_row[h] = jnp.where(jnp.zeros((1, 128), jnp.int32) + odd == 1, swap(row), row)

    loads[3].wait()
    loads[4].wait()
    def first_key(h):
        return ck_in[64 * h : 64 * h + 64, 0:128].astype(F32)[:, 0:1]

    spare = [jnp.broadcast_to(first_key(h), (64, 128)) for h in range(HL)]

    def cache(i, _):
        lanes = pl.ds(pl.multiple_of(i * 128, 128), 128)
        valid = lax.broadcasted_iota(jnp.int32, (64, 128), 1) + i * 128 < plen_ref[0]
        one = jnp.where(valid, 1.0, 0.0).astype(BF)
        for h in range(HL):
            k = ck_in[64 * h : 64 * h + 64, lanes].astype(F32)
            v = cv_in[64 * h : 64 * h + 64, lanes].astype(F32)
            k = jnp.where(valid, k, spare[h]).astype(BF)
            kx[h, 0, 0:64, lanes] = k
            kx[h, 0, 64:128, lanes] = k
            vx[h, 0, 0:64, lanes] = jnp.where(valid, v, 0.0).astype(BF)
            vx[h, 0, 64:128, lanes] = one
        return 0

    lax.fori_loop(0, ROWS // 128, cache, 0)
    used = jnp.zeros((64, ROWS), jnp.int32) + g > newest
    one = jnp.where(used, 1.0, 0.0).astype(BF)
    for h in range(HL):
        vx[h, 1, 64:128, :] = jnp.ones((64, ROWS), BF)
        vx[h, 2, 64:128, :] = one

    def clear(h, _):
        acc_ref[h] = jnp.zeros((ROWS, 128), F32)
        max_ref[h] = jnp.full((ROWS, 128), NEG, F32)
        return 0

    lax.fori_loop(0, HL, clear, 0)

    def take_queries(h):
        wait_bytes(q_got.at[h, pl.ds(0, N - 1)], qr.at[h])
        mask = low_lanes((64, 128))

        def body(n, _):
            for b in range(4):
                b = n * 4 + b
                x = q_got[h, b].astype(F32) * SCALE
                r = swap(x)
                qx[h, b, 0:64] = jnp.where(mask, x, r - r.astype(BF).astype(F32)).astype(BF)
                qx[h, b, 64:128] = jnp.where(mask, r, x - x.astype(BF).astype(F32)).astype(BF)
            return 0

        lax.fori_loop(0, N // 4, body, 0)

    def take_own(h):
        wait_bytes(kv_got.at[h, pl.ds(0, N - 1)], kvr.at[h])
        for b in range(N):
            lanes = slice(b * TB, (b + 1) * TB)
            k = kv_got[h, b, 0:64]
            kx[h, 1, 0:64, lanes] = k
            kx[h, 1, 64:128, lanes] = k
            vx[h, 1, 0:64, lanes] = kv_got[h, b, 64:128]

    def take_newest(h):
        wait_bytes(span_got.at[h, 0], r4.at[h])
        used = jnp.zeros((64, 128), jnp.int32) + g > newest
        spare = jnp.broadcast_to(kx[h, 0, 0:64, 0:128].astype(F32)[:, 0:1], (64, 128))
        for b in range(N):
            lanes = slice(b * TB, (b + 1) * TB)
            k = jnp.where(used, span_got[h, b % 2, b // 2, 0:64].astype(F32), spare).astype(BF)
            v = jnp.where(used, span_got[h, b % 2, b // 2, 64:128].astype(F32), 0.0).astype(BF)
            kx[h, 2, 0:64, lanes] = k
            kx[h, 2, 64:128, lanes] = k
            vx[h, 2, 0:64, lanes] = v

    def window(s):
        return pl.ds(pl.multiple_of(lax.div(s * HL, 2) * 128, 128), 256)

    def pick_newest():
        wait_bytes(near.at[pl.ds(0, N // 2 - 1)], r1)

        def choose(n, _):
            lanes = pl.ds(pl.multiple_of(n * 512, 512), 512)
            kept = jnp.zeros((16, 512), F32)
            for j in range(N // 2):
                chosen = jnp.zeros((16, 512), jnp.int32) + lax.div(newest, 2) == j
                kept = jnp.where(chosen, near[j, :, lanes].astype(F32), kept)
            pick[:, lanes] = kept.astype(BF)
            return 0

        lax.fori_loop(0, D // 512, choose, 0)
        part[sp] = pick[:, window(sp)]
        to_sp(lambda to: pick.at[:, window(to)], part.at[sp], s2, r2)

    def spread_newest():
        wait_bytes(part.at[pl.ds(0, N - 1)], r2)
        x = part[...].astype(F32)
        k = x[:, :8].reshape(TB, 256)
        v = x[:, 8:].reshape(TB, 256)
        odd = jnp.zeros((TB, 64), jnp.int32) + lax.rem(sp, 2) == 1

        def piece(y, h):
            return jnp.where(odd, y[:, 64 * (h + 1) : 64 * (h + 2)], y[:, 64 * h : 64 * (h + 1)])

        for h in range(HL):
            value = jnp.concatenate([piece(k, h), piece(v, h)], axis=1).T.astype(BF)
            span_pack[h] = value
            span_got[h, core, chip] = value
        for h in range(HL):
            to_chips(lambda to: span_pack.at[h], span_got.at[h, core, chip], s3.at[h], r3.at[h])

    def forward(h):
        wait_bytes(span_got.at[h, core, pl.ds(0, N // 2 - 1)], r3.at[h])
        to_mate(span_got.at[h, core], span_got.at[h, core], s4.at[h], r4.at[h])

    def attend(h, seg, last):
        def block(i, _):
            rows = pl.ds(pl.multiple_of(i * BQ, BQ), BQ)
            blocks = pl.ds(pl.multiple_of(i * (BQ // TB), BQ // TB), BQ // TB)
            q = qx[h, blocks].reshape(BQ, 128)
            m = max_ref[h, rows, :]
            acc = acc_ref[h, rows, :]
            s = jnp.dot(q, kx[h, seg], preferred_element_type=F32)
            top = jnp.maximum(m, jnp.broadcast_to(jnp.max(s, axis=1, keepdims=True), (BQ, 128)))
            w = jnp.exp2(s - jnp.tile(top, (1, ROWS // 128))).astype(BF)
            new = lax.dot_general(w, vx[h, seg], (((1,), (1,)), ((), ())), preferred_element_type=F32)
            max_ref[h, rows, :] = top
            acc_ref[h, rows, :] = acc * jnp.exp2(m - top) + new

            @pl.when(last)
            def _():
                done = acc_ref[h, rows, :]
                gated = (done / swap(done) * gate_row[h]).reshape(BQ // TB, TB, 128)
                mask = low_lanes((BQ // TB, 64, 128))
                out_pack[h, blocks] = jnp.where(mask, gated[:, :64], swap(gated[:, 64:])).astype(BF)

                def send(b, _):
                    to = i * (BQ // TB) + b

                    @pl.when(to != sp)
                    def _():
                        pltpu.make_async_remote_copy(
                            src_ref=out_pack.at[h, to], dst_ref=out_got.at[h, sp],
                            send_sem=os.at[h], recv_sem=orr.at[h],
                            device_id={"sp": to}, device_id_type=MESH,
                        ).start()

                    @pl.when(to == sp)
                    def _():
                        out_got[h, sp] = out_pack[h, sp]

                    return 0

                lax.fori_loop(0, BQ // TB, send, 0)

            return 0

        lax.fori_loop(0, ROWS // BQ, block, 0)

    order = [(0, 0), (0, 1), (1, 0), (2, 0), (0, 2), (1, 1), (1, 2), (2, 2), (2, 1)]

    def step(i, _):
        @pl.when(i == PICK)
        def _():
            pick_newest()
            send_kv(1)
            send_kv(2)

        @pl.when(i == SPREAD)
        def _():
            spread_newest()

        for n, heads in FORWARD.items():
            @pl.when(i == n)
            def _():
                for h in heads:
                    forward(h)

        h = jnp.int32(0)
        seg = jnp.int32(0)
        for n, (hn, sn) in enumerate(order):
            h = jnp.where(i == n, hn, h)
            seg = jnp.where(i == n, sn, seg)

        @pl.when(seg == 0)
        def _():
            take_queries(h)

        @pl.when(seg == 1)
        def _():
            take_own(h)

        @pl.when(seg == 2)
        def _():
            take_newest(h)

        last = jnp.logical_or(i == 4, jnp.logical_or(i == 6, i == 8))
        attend(h, seg, last)
        return 0

    lax.fori_loop(0, len(order), step, 0)

    low = low_lanes((64, 128))

    def assemble(t):
        j = 2 * t
        a = out_got[j % HL, j // HL].astype(F32)
        b = out_got[(j + 1) % HL, (j + 1) // HL].astype(F32)
        cols = slice(t * 128, (t + 1) * 128)
        o_ref[0, 0:64, cols] = jnp.where(low, a, swap(b)).astype(BF)
        o_ref[0, 64:128, cols] = jnp.where(low, swap(a), b).astype(BF)

    for h in range(HL):
        wait_bytes(out_got.at[h, pl.ds(0, N - 1)], orr.at[h])
        if h == 1:
            for t in range(0, D // 128, 3):
                assemble(t)
    for t in range(D // 128):
        if t % 3:
            assemble(t)

    wait_bytes(mate, s0)
    wait_bytes(mine.at[pl.ds(0, N // 2 - 1)], s1)
    wait_bytes(part.at[pl.ds(0, N - 1)], s2)
    for h in range(HL):
        wait_bytes(q_pack.at[h, pl.ds(0, N - 1)], qs.at[h])
        wait_bytes(kv_pack.at[h, pl.ds(0, N - 1)], kvs.at[h])
        wait_bytes(span_got.at[h, 0, pl.ds(0, N // 2 - 1)], s3.at[h])
        wait_bytes(span_got.at[h, 0], s4.at[h])
        wait_bytes(out_pack.at[h, pl.ds(0, N - 1)], os.at[h])


def per_device(queries, keys, values, cache_keys, cache_values, *rest):
    args = (queries, keys, values, cache_keys.swapaxes(1, 2), cache_values.swapaxes(1, 2), *rest)
    any_ = pl.BlockSpec(memory_space=pl.ANY)
    smem = pl.BlockSpec(memory_space=pltpu.SMEM)
    V = pltpu.VMEM
    dma = pltpu.SemaphoreType.DMA
    return pl.pallas_call(
        kernel,
        out_shape=jax.ShapeDtypeStruct((1, TB, D), BF),
        in_specs=[any_] * 6 + [smem] * 3,
        out_specs=pl.BlockSpec(memory_space=pltpu.VMEM),
        scratch_shapes=[
            V((TB, D), BF), V((TB, D), BF), V((TB, D), BF),
            V((HL * 64, ROWS), BF), V((HL * 64, ROWS), BF), V((64, D), F32), V((HL, 1, 128), F32),
            V((HL, N, 64, 128), BF), V((HL, N, TB, 128), BF),
            V((HL, N, 64, 128), BF), V((HL, N, TB, 128), BF),
            V((2, N // 2, 16, D), BF), V((N // 2, 16, D), BF), V((N // 2, 16, D), BF),
            V((N // 2, 16, D), BF), V((16, D), BF), V((N, 16, 256), BF),
            V((HL, TB, 128), BF), V((HL, 2, N // 2, TB, 128), BF),
            V((HL, N, TB, 128), BF), V((HL, 3, 128, ROWS), BF), V((HL, 3, 128, ROWS), BF),
            V((HL, ROWS, 128), F32), V((HL, ROWS, 128), F32),
            V((HL, N, 64, 128), BF), V((HL, N, 64, 128), BF),
            dma((6,)), dma((HL,)), dma((HL,)), dma((HL,)), dma((HL,)),
            dma, dma, dma, dma, dma, dma, dma((HL,)), dma((HL,)), dma((HL,)), dma((HL,)), dma((HL,)), dma((HL,)),
        ],
        compiler_params=pltpu.CompilerParams(
            collective_id=0, has_side_effects=True, vmem_limit_bytes=60 * 2**20
        ),
        cost_estimate=pl.CostEstimate(
            flops=9 * 2 * 2 * ROWS * ROWS * 64, bytes_accessed=6 * 2**20,
            transcendentals=9 * ROWS * ROWS,
        ),
    )(*args)


def solution(mesh):
    placed = (
        P("span", "sp", None),
        P("span", "sp", None),
        P("span", "sp", None),
        P("span", None, "sp"),
        P("span", None, "sp"),
        P(),
        P("span"),
        P("span"),
        P(),
    )
    return jax.shard_map(
        per_device, mesh=mesh, in_specs=placed, out_specs=P("span", "sp", None), check_vma=False
    )
```
